32 devices in a mesh: uly: 4 (over y, x), blk: 8 (over z, core).
Axes of the slice: x: 2, y: 2, z: 4, core: 2. Of those that a mesh axis runs over, the one named last changes fastest.
Arguments:
- video_q: bfloat16 [9216, 3072], P(('blk', 'uly')), may hold values from -16 to 16
- video_k: bfloat16 [9216, 3072], P(('blk', 'uly')), may hold values from -16 to 16
- video_v: bfloat16 [9216, 3072], P(('blk', 'uly')), may hold values from -6 to 6
- text_q: bfloat16 [256, 3072], P('uly'), may hold values from -16 to 16
- text_k: bfloat16 [256, 3072], P('uly'), may hold values from -16 to 16
- text_v: bfloat16 [256, 3072], P('uly'), may hold values from -6 to 6
- window_tiles: int32 [24, 6], P('blk'), may hold values from 0 to 23, as said below
- text_len: int32 [1], replicated, may hold values from 64 to 256
Outputs:
- video_out: bfloat16 [9216, 3072], P(('blk', 'uly'))
- text_out: bfloat16 [256, 3072], P('uly')
The draws below stay inside these ranges and needn't reach their ends.
Inputs may be any that keep to these rules, and one draw needn't show every extreme that they name: `window_tiles`: tile j lies in time slice j // 3 of 8; row j lists, each once and in any order, the 6 tiles of two consecutive time slices, one of which is the slice of tile j.
All inputs are finite; a program needn't handle non-finite values.
Results may differ from the reference program's by a relative error of at most 0.0036.
Values may be sent and summed in bfloat16 or wider, within the bound.
A program may use at most 128 MiB of HBM per device.

```python
import math
import jax
import jax.numpy as jnp
from jax import lax

HEADS = 24
D_HEAD = 128
TXT = 256
TILE = 384
TW_DEV = 3
WIN = 6
QTILES = 24
TSLICES = 8
VID = 9216


def lifted(key, row_count, col_count, label):
    spread = 1.6
    base = jax.random.fold_in(key, label)
    noise = jax.random.normal(jax.random.fold_in(base, 14), (row_count, col_count), jnp.float32)
    return spread * jnp.clip(noise, -6.0, 6.0)


def draw_video_q(key, part):
    return lifted(key, VID, HEADS * D_HEAD, 101).astype(jnp.bfloat16)


def draw_video_k(key, part):
    return lifted(key, VID, HEADS * D_HEAD, 202).astype(jnp.bfloat16)


def draw_text_q(key, part):
    return lifted(key, TXT, HEADS * D_HEAD, 303).astype(jnp.bfloat16)


def draw_text_k(key, part):
    return lifted(key, TXT, HEADS * D_HEAD, 404).astype(jnp.bfloat16)


def draw_window_tiles(key, part):
    positions = jnp.arange(QTILES, dtype=jnp.int32)
    time_slice = positions // TW_DEV
    coin_flip = jax.random.randint(jax.random.fold_in(key, 21), (QTILES,), 0, 2)
    first_slice = jnp.clip(time_slice - coin_flip, 0, TSLICES - 2)
    member = first_slice[:, None] * TW_DEV + jnp.arange(WIN, dtype=jnp.int32)[None, :]
    scores = jax.random.randint(jax.random.fold_in(key, 22), (QTILES, WIN), 0, 1 << 20) * WIN
    scores = scores + jnp.arange(WIN, dtype=jnp.int32)[None, :]
    ordering = jnp.argsort(scores, axis=1)
    return jnp.take_along_axis(member, ordering, axis=1).astype(jnp.int32)


def block_scale(stream_key, dims, shards, low, top_value):
    def one(position, shards_of):
        heights = jax.random.uniform(jax.random.fold_in(jax.random.fold_in(stream_key, 6), position), (shards_of,), jnp.float32, low / len(shards), top_value / len(shards))
        return jnp.repeat(jnp.exp(heights), dims[position] // shards_of).reshape((-1,) + (1,) * (len(dims) - position - 1))

    gain = one(*shards[0])
    for cut in shards[1:]:
        gain = gain * one(*cut)
    return gain


def gaussian(rng, shape, width, bound, split=(), kind=jnp.bfloat16):
    array = jax.random.normal(rng, shape, jnp.float32) * width
    if len(split) > 0:
        array = block_scale(rng, shape, split, -0.22, 0.18) * array
    return jnp.clip(array, min=-bound, max=bound).astype(kind)


def setup_inputs(seed: int = 0) -> dict:
    seeds = jax.random.split(jax.random.key(seed), 9)
    return {
        "video_q": draw_video_q(jax.random.fold_in(seeds[8], 71), 0),
        "video_k": draw_video_k(jax.random.fold_in(seeds[8], 71), 0),
        "video_v": gaussian(seeds[2], (VID, HEADS * D_HEAD), 1.0, 6.0, ((0, 32),)),
        "text_q": draw_text_q(jax.random.fold_in(seeds[8], 71), 0),
        "text_k": draw_text_k(jax.random.fold_in(seeds[8], 71), 0),
        "text_v": gaussian(seeds[5], (TXT, HEADS * D_HEAD), 1.0, 6.0, ((0, 4),)),
        "window_tiles": draw_window_tiles(jax.random.fold_in(seeds[8], 71), 0),
        "text_len": jax.random.randint(seeds[7], (1,), TXT // 4, TXT + 1).astype(jnp.int32),
    }


def round_bf(values):
    rounded = lax.optimization_barrier(values.astype(jnp.bfloat16))
    return rounded.astype(jnp.float32)

def reference(video_q, video_k, video_v, text_q, text_k, text_v, window_tiles, text_len):
    inv_root = 1.0 / math.sqrt(D_HEAD)
    tile_q = video_q.reshape(QTILES, TILE, HEADS, D_HEAD)
    tile_k = video_k.reshape(QTILES, TILE, HEADS, D_HEAD)
    tile_v = video_v.reshape(QTILES, TILE, HEADS, D_HEAD)
    text_keys = text_k.reshape(TXT, HEADS, D_HEAD).astype(jnp.float32)
    text_values = text_v.reshape(TXT, HEADS, D_HEAD).astype(jnp.float32)
    live_text = jnp.arange(TXT, dtype=jnp.int32) < text_len[0]

    def tile_attention(inputs):
        queries, chosen = inputs
        keys_win = jnp.take(tile_k, chosen, axis=0).reshape(WIN * TILE, HEADS, D_HEAD).astype(jnp.float32)
        values_win = jnp.take(tile_v, chosen, axis=0).reshape(WIN * TILE, HEADS, D_HEAD).astype(jnp.float32)
        queries_wide = queries.astype(jnp.float32)
        win_scores = jnp.einsum('qhd,khd->hqk', queries_wide, keys_win) * inv_root
        txt_scores = jnp.einsum('qhd,khd->hqk', queries_wide, text_keys) * inv_root
        txt_scores = jnp.where(live_text[None, None, :], txt_scores, -jnp.inf)
        row_top = jnp.maximum(lax.optimization_barrier(jnp.max(win_scores, axis=2)), lax.optimization_barrier(jnp.max(txt_scores, axis=2)))[:, :, None]
        win_weights = jnp.exp(win_scores - row_top)
        txt_weights = jnp.exp(txt_scores - row_top)
        weight_sum = lax.optimization_barrier(jnp.sum(win_weights, axis=2)) + lax.optimization_barrier(jnp.sum(txt_weights, axis=2))
        numerator = jnp.einsum('hqk,khd->hqd', round_bf(win_weights), values_win)
        numerator = numerator + jnp.einsum('hqk,khd->hqd', round_bf(txt_weights), text_values)
        result = numerator / weight_sum[:, :, None]
        return jnp.transpose(result, (1, 0, 2)).astype(jnp.bfloat16)
    video_out = lax.map(tile_attention, (tile_q, window_tiles)).reshape(VID, HEADS * D_HEAD)

    def text_attention(inputs):
        queries, keys_vid, values_vid, keys_txt, values_txt = inputs
        vid_scores = jnp.dot(queries, keys_vid.T, preferred_element_type=jnp.float32) * inv_root
        txt_scores = jnp.dot(queries, keys_txt.T, preferred_element_type=jnp.float32) * inv_root
        txt_scores = jnp.where(live_text[None, :], txt_scores, -jnp.inf)
        row_top = jnp.maximum(lax.optimization_barrier(jnp.max(vid_scores, axis=1)), lax.optimization_barrier(jnp.max(txt_scores, axis=1)))[:, None]
        vid_weights = jnp.exp(vid_scores - row_top)
        txt_weights = jnp.exp(txt_scores - row_top)
        weight_sum = lax.optimization_barrier(jnp.sum(vid_weights, axis=1)) + lax.optimization_barrier(jnp.sum(txt_weights, axis=1))
        numerator = jnp.dot(vid_weights.astype(jnp.bfloat16), values_vid, preferred_element_type=jnp.float32)
        numerator = numerator + jnp.dot(txt_weights.astype(jnp.bfloat16), values_txt, preferred_element_type=jnp.float32)
        return (numerator / weight_sum[:, None]).astype(jnp.bfloat16)
    per_head = (jnp.transpose(text_q.reshape(TXT, HEADS, D_HEAD), (1, 0, 2)), jnp.transpose(video_k.reshape(VID, HEADS, D_HEAD), (1, 0, 2)), jnp.transpose(video_v.reshape(VID, HEADS, D_HEAD), (1, 0, 2)), jnp.transpose(text_k.reshape(TXT, HEADS, D_HEAD), (1, 0, 2)), jnp.transpose(text_v.reshape(TXT, HEADS, D_HEAD), (1, 0, 2)))
    text_heads = lax.map(text_attention, per_head)
    text_out = jnp.transpose(text_heads, (1, 0, 2)).reshape(TXT, HEADS * D_HEAD)
    return (video_out, text_out)
```

```python
import functools
import math

import jax
import jax.numpy as jnp
from jax import lax
from jax.experimental import pallas as pl
from jax.experimental.pallas import tpu as pltpu
from jax.sharding import PartitionSpec as P

D = 128
TILE = 384
PIECE = 32
MESH = pl.DeviceIdType.MESH
NEG = -jnp.inf
SCALE = math.log2(math.e) / math.sqrt(D)


def dot_t(a, b):
    return lax.dot_general(a, b, (((1,), (1,)), ((), ())), preferred_element_type=jnp.float32)


def dot(a, b):
    return jnp.dot(a, b, preferred_element_type=jnp.float32)


def kernel(
    n_u, n_b, heads, rows, trows,
    vq, vk, vv, tq, tk, tv, win, tlen,
    vout, tout,
    qb, kb, vb, kp, vp, kn, vn, ob, tqb, tkb, tvb, po, pml, ro, rml, fin,
    xs, xr, ts, tr, hs, hr, os_, or_, ps, pr, fs, fr,
):
    u = lax.axis_index("uly")
    b = lax.axis_index("blk")
    width = heads * D
    tiles = n_u * rows // TILE
    text = n_u * trows
    pieces = text // PIECE
    per_u = trows // PIECE
    has_prev = b > 0
    has_next = b < n_b - 1

    def to_uly(r):
        return lax.rem(u + r, n_u)

    def from_uly(r):
        return lax.rem(u + n_u - r, n_u)

    def remote(src, dst, s, r, uly, blk):
        return pltpu.make_async_remote_copy(
            src_ref=src, dst_ref=dst, send_sem=s, recv_sem=r,
            device_id=(blk, uly) if AXES[0] == "blk" else (uly, blk), device_id_type=MESH,
        )

    video = ((vk, kb), (vv, vb), (vq, qb))
    texts = ((tq, tqb), (tk, tkb), (tv, tvb))

    def x_copy(i, h, r, dest, src):
        a, buf = video[i]
        source = a.at[:, pl.ds(pl.multiple_of((dest * heads + h) * D, D), D)]
        target = buf.at[h, pl.ds(pl.multiple_of(src * rows, 16), rows), :]
        return source, target, xs.at[i, h, r], xr.at[i, h, r]

    def x_start(i, h):
        for r in range(1, n_u):
            remote(*x_copy(i, h, r, to_uly(r), u), to_uly(r), b).start()
        s, t, _, sem = x_copy(i, h, 0, u, u)
        pltpu.make_async_copy(s, t, sem).start()

    def x_wait(i, h):
        s, t, _, sem = x_copy(i, h, 0, u, u)
        pltpu.make_async_copy(s, t, sem).wait()
        for r in range(1, n_u):
            remote(*x_copy(i, h, r, to_uly(r), from_uly(r)), to_uly(r), b).wait_recv()

    def t_copy(i, r, dest, src):
        a, buf = texts[i]
        source = a.at[:, pl.ds(pl.multiple_of(dest * width, D), width)]
        target = buf.at[pl.ds(pl.multiple_of(src * trows, 16), trows), :]
        return source, target, ts.at[i, r], tr.at[i, r]

    def halo(h, i):
        src = (kb, vb)[i % 2]
        dst = (kp, vp, kn, vn)[i]
        blk = b + 1 if i < 2 else b - 1
        return remote(src.at[h], dst.at[h], hs.at[h, i], hr.at[h, i], u, blk)

    def halo_each(h, first, second, what):
        for cond, ids in ((first, (0, 1)), (second, (2, 3))):
            @pl.when(cond)
            def _():
                for i in ids:
                    what(halo(h, i))

    def o_copy(h, r, dest, src):
        source = ob.at[h, pl.ds(pl.multiple_of(dest * rows, 16), rows), :]
        target = vout.at[:, pl.ds(pl.multiple_of((src * heads + h) * D, D), D)]
        return source, target, os_.at[h, r], or_.at[h, r]

    for i in range(3):
        for r in range(1, n_u):
            remote(*t_copy(i, r, to_uly(r), u), to_uly(r), b).start()
        s, t, _, sem = t_copy(i, 0, u, u)
        pltpu.make_async_copy(s, t, sem).start()

    def start_head(h, c):
        for i in range(3):
            x_start(i, h)
        return c

    lax.fori_loop(0, heads, start_head, 0)

    for i in range(3):
        s, t, _, sem = t_copy(i, 0, u, u)
        pltpu.make_async_copy(s, t, sem).wait()
        for r in range(1, n_u):
            remote(*t_copy(i, r, to_uly(r), from_uly(r)), to_uly(r), b).wait_recv()

    live = tlen[0]
    lane = lax.broadcasted_iota(jnp.int32, (1, text), 1)
    video_bias = jnp.where(lane < live, 0.0, NEG)
    text_bias = jnp.where(lane < jnp.where(b == 0, live, 0), 0.0, NEG)
    lane8 = lax.broadcasted_iota(jnp.int32, (1, D), 1) // 8

    def arrive(h):
        x_wait(0, h)
        x_wait(1, h)
        halo_each(h, has_next, has_prev, lambda c: c.start())
        cols = pl.ds(pl.multiple_of(h * D, D), D)
        q = tqb[:, cols]
        s1 = dot_t(q, kb[h])
        s2 = dot_t(q, tkb[:, cols]) + text_bias
        m = jnp.maximum(jnp.max(s1, axis=1, keepdims=True), jnp.max(s2, axis=1, keepdims=True))
        p1 = jnp.exp2((s1 - m) * SCALE)
        p2 = jnp.exp2((s2 - m) * SCALE)
        total = jnp.sum(p1, axis=1, keepdims=True) + jnp.sum(p2, axis=1, keepdims=True)
        o = dot(p1.astype(jnp.bfloat16), vb[h]) + dot(p2.astype(jnp.bfloat16), tvb[:, cols])
        po[h] = o.astype(jnp.bfloat16)
        pml[...] = jnp.where(lane8 == 2 * h, m, jnp.where(lane8 == 2 * h + 1, total, pml[...]))

    def attend(h):
        x_wait(2, h)
        halo_each(h, has_prev, has_next, lambda c: c.wait_recv())
        cols = pl.ds(pl.multiple_of(h * D, D), D)

        def tile(t, c):
            last = win[t, 0]
            for w in range(1, win.shape[1]):
                last = jnp.maximum(last, win[t, w])
            after = last >= (b + 1) * tiles
            at = pl.ds(pl.multiple_of(t * TILE, 16), TILE)
            q = qb[h, at, :]
            s1 = dot_t(q, kb[h])
            s2 = dot_t(q, jnp.where(after, kn[h], kp[h]))
            s3 = dot_t(q, tkb[:, cols]) + video_bias
            m = jnp.maximum(jnp.max(s1, axis=1, keepdims=True), jnp.max(s2, axis=1, keepdims=True))
            m = jnp.maximum(m, jnp.max(s3, axis=1, keepdims=True))
            p1 = jnp.exp2((s1 - m) * SCALE)
            p2 = jnp.exp2((s2 - m) * SCALE)
            p3 = jnp.exp2((s3 - m) * SCALE)
            total = (
                jnp.sum(p1, axis=1, keepdims=True)
                + jnp.sum(p2, axis=1, keepdims=True)
                + jnp.sum(p3, axis=1, keepdims=True)
            )
            o = dot(p1.astype(jnp.bfloat16), vb[h])
            o = o + dot(p2.astype(jnp.bfloat16), jnp.where(after, vn[h], vp[h]))
            o = o + dot(p3.astype(jnp.bfloat16), tvb[:, cols])
            ob[h, at, :] = (o / total).astype(jnp.bfloat16)
            return c

        lax.fori_loop(0, tiles, tile, 0)
        for r in range(1, n_u):
            remote(*o_copy(h, r, to_uly(r), u), to_uly(r), b).start()
        s, t, _, sem = o_copy(h, 0, u, u)
        pltpu.make_async_copy(s, t, sem).start()

    def p_copies(r, dest, src):
        at = pl.ds(pl.multiple_of(dest * PIECE, PIECE), PIECE)
        return (
            (po.at[:, at, :], ro.at[src], ps.at[0, r], pr.at[0, r]),
            (pml.at[at, :], rml.at[src], ps.at[1, r], pr.at[1, r]),
        )

    def to_blk(r):
        return lax.rem(b + r, n_b)

    def from_blk(r):
        return lax.rem(b + n_b - r, n_b)

    def p_start():
        for r in range(1, n_b):
            @pl.when(to_blk(r) < pieces)
            def _():
                for c in p_copies(r, to_blk(r), b):
                    remote(*c, u, to_blk(r)).start()
        @pl.when(b < pieces)
        def _():
            for s, t, _, sem in p_copies(0, b, b):
                pltpu.make_async_copy(s, t, sem).start()

    owner = b // per_u
    my_rows = pl.ds(pl.multiple_of(lax.rem(b, per_u) * PIECE, PIECE), PIECE)

    def f_out(r):
        slot = u * per_u + lax.rem(b, per_u)
        target = tout.at[my_rows, pl.ds(pl.multiple_of(u * width, D), width)]
        return (fin, target, fs.at[r], fr.at[slot])

    def f_each(what_remote, what_local):
        for r in range(n_b):
            if r == 0:
                @pl.when(owner == u)
                def _():
                    if what_local is not None:
                        s, t, _, sem = f_out(0)
                        what_local(pltpu.make_async_copy(s, t, sem))

                @pl.when(owner != u)
                def _():
                    what_remote(remote(*f_out(0), owner, b))
            else:
                what_remote(remote(*f_out(r), owner, to_blk(r)))

    def merge():
        for r in range(1, n_b):
            for c in p_copies(r, b, from_blk(r)):
                remote(*c, u, to_blk(r)).wait_recv()
        for s, t, _, sem in p_copies(0, b, b):
            pltpu.make_async_copy(s, t, sem).wait()
        ml = rml[...]
        lanes = lane8[None]
        for h in range(heads):
            m = jnp.max(jnp.where(lanes == 2 * h, ml, NEG), axis=2, keepdims=True)
            total = jnp.max(jnp.where(lanes == 2 * h + 1, ml, 0.0), axis=2, keepdims=True)
            w = jnp.exp2((m - jnp.max(m, axis=0, keepdims=True)) * SCALE)
            o = jnp.sum(ro[:, h].astype(jnp.float32) * w, axis=0)
            fin[:, h * D:(h + 1) * D] = (o / jnp.sum(total * w, axis=0)).astype(jnp.bfloat16)
        f_each(lambda c: c.start(), lambda c: c.start())

    pml[...] = jnp.zeros_like(pml)
    arrive(0)

    def step(h, c):
        @pl.when(h < heads - 1)
        def _():
            arrive(h + 1)

        @pl.when(h == heads - 2)
        def _():
            p_start()

        @pl.when(h == heads - 1)
        def _():
            pl.when(b < pieces)(merge)

        attend(h)
        return c

    lax.fori_loop(0, heads, step, 0)

    def finish(h, c):
        s, t, _, sem = o_copy(h, 0, u, u)
        pltpu.make_async_copy(s, t, sem).wait()
        for r in range(1, n_u):
            remote(*o_copy(h, r, to_uly(r), from_uly(r)), to_uly(r), b).wait_recv()
            remote(*o_copy(h, r, to_uly(r), u), to_uly(r), b).wait_send()
            for i in range(3):
                remote(*x_copy(i, h, r, to_uly(r), u), to_uly(r), b).wait_send()
        halo_each(h, has_next, has_prev, lambda c: c.wait_send())
        return c

    lax.fori_loop(0, heads, finish, 0)
    for i in range(3):
        for r in range(1, n_u):
            remote(*t_copy(i, r, to_uly(r), u), to_uly(r), b).wait_send()
    for r in range(1, n_b):
        @pl.when(to_blk(r) < pieces)
        def _():
            for c in p_copies(r, to_blk(r), b):
                remote(*c, u, to_blk(r)).wait_send()

    @pl.when(b < pieces)
    def _():
        f_each(lambda c: c.wait_send(), None)

    for su in range(n_u):
        for k in range(per_u):
            slot = su * per_u + k
            target = tout.at[k * PIECE:(k + 1) * PIECE, su * width:(su + 1) * width]
            pltpu.make_async_copy(fin, target, fr.at[slot]).wait()


AXES = ["uly", "blk"]


def local(n_u, n_b, *args):
    vq, _, _, tq = args[:4]
    rows, cols = vq.shape
    trows = tq.shape[0]
    heads = cols // D // n_u
    seq, text = rows * n_u, trows * n_u
    bf = jnp.bfloat16
    dma = pltpu.SemaphoreType.DMA
    slab = pltpu.VMEM((heads, seq, D), bf)
    tslab = pltpu.VMEM((text, heads * D), bf)
    hbm = pl.BlockSpec(memory_space=pl.ANY)
    smem = pl.BlockSpec(memory_space=pltpu.SMEM)
    slots = n_u * (trows // PIECE)
    return pl.pallas_call(
        functools.partial(kernel, n_u, n_b, heads, rows, trows),
        out_shape=(
            jax.ShapeDtypeStruct((rows, cols), bf),
            jax.ShapeDtypeStruct((trows, cols), bf),
        ),
        in_specs=[hbm] * 6 + [smem] * 2,
        out_specs=(hbm, hbm),
        scratch_shapes=[slab] * 8 + [tslab] * 3 + [
            pltpu.VMEM((heads, text, D), bf),
            pltpu.VMEM((text, D), jnp.float32),
            pltpu.VMEM((n_b, heads, PIECE, D), bf),
            pltpu.VMEM((n_b, PIECE, D), jnp.float32),
            pltpu.VMEM((PIECE, heads * D), bf),
            dma((3, heads, n_u)), dma((3, heads, n_u)),
            dma((3, n_u)), dma((3, n_u)),
            dma((heads, 4)), dma((heads, 4)),
            dma((heads, n_u)), dma((heads, n_u)),
            dma((2, n_b)), dma((2, n_b)),
            dma((n_b,)), dma((slots,)),
        ],
        compiler_params=pltpu.CompilerParams(
            has_side_effects=True, vmem_limit_bytes=56 * 2**20
        ),
    )(*args)


def solution(mesh):
    AXES[:] = mesh.axis_names
    in_specs = (
        P(("blk", "uly"), None),
        P(("blk", "uly"), None),
        P(("blk", "uly"), None),
        P("uly", None),
        P("uly", None),
        P("uly", None),
        P("blk", None),
        P(),
    )
    out_specs = (P(("blk", "uly"), None), P("uly", None))
    body = functools.partial(local, mesh.shape["uly"], mesh.shape["blk"])
    return jax.shard_map(body, mesh=mesh, in_specs=in_specs, out_specs=out_specs, check_vma=False)
```
